32 devices in a mesh: phase: 2 (over x), blk: 4 (over z), tp: 4 (over y, core).
Axes of the slice: x: 2, y: 2, z: 4, core: 2. Of those that a mesh axis runs over, the one named last changes fastest.
Arguments:
- grid_lat: bfloat16 [8192, 512], P(('phase', 'blk')), may hold values from -6 to 6
- mesh_lat: bfloat16 [4096, 512], P('blk'), may hold values from -6 to 6
- mesh_cot: bfloat16 [4096, 512], P('blk'), may hold values from -6 to 6
- edge_lat: bfloat16 [4, 8192, 512], P(None, ('phase', 'blk')), may hold values from -6 to 6
- edge_slot: int32 [4, 8192], P(None, ('phase', 'blk')), may hold values from 0 to 127
- serve_list: int32 [2, 4, 4, 32], P('phase', 'blk'), may hold values from 0 to 1023
- w_grid: bfloat16 [512, 512], P('tp'), may hold values from -0.25 to 0.25
- w_mesh: bfloat16 [512, 512], P('tp'), may hold values from -0.25 to 0.25
- w_edge: bfloat16 [512, 512], P('tp'), may hold values from -0.25 to 0.25
- w_out: bfloat16 [512, 512], P('tp'), may hold values from -0.25 to 0.25
- bias: float32 [512], P('tp'), may hold values from -4 to 4
Outputs:
- grid_grad: bfloat16 [8192, 512], P(('phase', 'blk'), 'tp')
- mesh_grad: bfloat16 [4096, 512], P('blk', 'tp')
The draws below stay inside these ranges and needn't reach their ends.
All inputs are finite; a program needn't handle non-finite values.
Results may differ from the reference program's by a relative error of at most 0.0051.
Values may be sent and summed in bfloat16 or wider, within the bound.
A program may use at most 64 MiB of HBM per device.

```python
import jax
import jax.numpy as jnp
from jax import lax

LAT = 512
HID = 512
EPG = 4
CAP = 32
GRID_DEV = 1024
GRID = 8192
MESH_DEV = 1024
MESH = 4096
SLOTS = 128
N_PHASE = 2
N_BLK = 4


def place_ends(entries, key, smallest, largest):
    spot = [jax.random.randint(jax.random.fold_in(key, axis), (), 0, length) for axis, length in enumerate(entries.shape)]
    longest = entries.shape.index(max(entries.shape))
    beside = spot[:longest] + [(spot[longest] + 1) % entries.shape[longest]] + spot[longest + 1:]
    return entries.at[tuple(spot)].set(smallest).at[tuple(beside)].set(largest)


def level_of(stream_key, dims, cuts, low, top_value):
    def one(dim, parts):
        steps = jax.random.uniform(jax.random.fold_in(jax.random.fold_in(stream_key, 6), dim), (parts,), jnp.float32, low / len(cuts), top_value / len(cuts))
        return jnp.repeat(jnp.exp(steps), dims[dim] // parts).reshape((-1,) + (1,) * (len(dims) - dim - 1))

    loudness = one(*cuts[0])
    for cut in cuts[1:]:
        loudness = loudness * one(*cut)
    return loudness


def gaussian(own_key, extent, scale, bound, split=(), kind=jnp.bfloat16):
    level = level_of(own_key, extent, split, -0.22, 0.18) if split else 1.0
    entries = jax.random.normal(own_key, extent, jnp.float32) * scale * level
    return jnp.minimum(jnp.maximum(entries, -bound), bound).astype(kind)


def setup_inputs(seed: int = 0) -> dict:
    seeds = jax.random.split(jax.random.key(seed), 12)
    grid_lat = gaussian(seeds[0], (GRID, LAT), 1.0, 6.0, ((0, 8),))
    mesh_lat = gaussian(seeds[1], (MESH, LAT), 1.0, 6.0, ((0, 4),))
    mesh_cot = gaussian(seeds[2], (MESH, LAT), 1.0, 6.0, ((0, 4),))
    edge_lat = gaussian(seeds[3], (EPG, GRID, LAT), 1.0, 6.0, ((1, 8),))
    edge_slot = place_ends(jax.random.randint(seeds[4], (EPG, GRID), 0, SLOTS), jax.random.fold_in(seeds[4], 1), 0, SLOTS - 1).astype(jnp.int32)
    serve_list = place_ends(jax.random.randint(seeds[5], (N_PHASE, N_BLK, N_BLK, CAP), 0, MESH_DEV), jax.random.fold_in(seeds[5], 1), 0, MESH_DEV - 1).astype(jnp.int32)
    w_grid = gaussian(seeds[6], (HID, LAT), LAT ** -0.5, 0.25, ((0, 4),))
    w_mesh = gaussian(seeds[7], (HID, LAT), LAT ** -0.5, 0.25, ((0, 4),))
    w_edge = gaussian(seeds[8], (HID, LAT), LAT ** -0.5, 0.25, ((0, 4),))
    w_out = gaussian(seeds[9], (HID, LAT), LAT ** -0.5, 0.25, ((0, 4),))
    bias = gaussian(seeds[10], (HID,), 0.7, 4.0, ((0, 4),), jnp.float32)
    return {"grid_lat": grid_lat, "mesh_lat": mesh_lat, "mesh_cot": mesh_cot, "edge_lat": edge_lat, "edge_slot": edge_slot, "serve_list": serve_list, "w_grid": w_grid, "w_mesh": w_mesh, "w_edge": w_edge, "w_out": w_out, "bias": bias}


def silu_slope(value):
    sigma = jax.nn.sigmoid(value)
    return sigma * (1.0 + value * (1.0 - sigma))


def reference(grid_lat, mesh_lat, mesh_cot, edge_lat, edge_slot, serve_list, w_grid, w_mesh, w_edge, w_out, bias):
    owner_count = N_PHASE * N_BLK
    mesh_pre = jnp.dot(mesh_lat, w_mesh.T, preferred_element_type=jnp.float32)
    act_grad = jnp.dot(mesh_cot, w_out.T, preferred_element_type=jnp.float32)
    offsets = (jnp.arange(N_BLK, dtype=jnp.int32) * MESH_DEV)[None, None, :, None]
    node_table = (jnp.transpose(serve_list, (0, 2, 1, 3)) + offsets).reshape(owner_count, SLOTS).astype(jnp.int32)
    grid_rows = grid_lat.reshape(owner_count, GRID_DEV, LAT)
    edge_rows = jnp.transpose(edge_lat.reshape(EPG, owner_count, GRID_DEV, LAT), (1, 0, 2, 3))
    slot_rows = jnp.transpose(edge_slot.reshape(EPG, owner_count, GRID_DEV), (1, 0, 2))
    bias_f = bias.astype(jnp.float32)

    def per_owner(collected, pieces):
        grid_part, edge_part, slot_part, node_list = pieces
        grid_pre = jnp.dot(grid_part, w_grid.T, preferred_element_type=jnp.float32)
        edge_pre = jnp.einsum("kgd,hd->kgh", edge_part.astype(jnp.float32), w_edge.astype(jnp.float32))
        node_ids = node_list[slot_part]
        preact = grid_pre[None] + mesh_pre[node_ids] + edge_pre + bias_f
        pre_grad = act_grad[node_ids] * silu_slope(preact)
        grid_sum = jnp.sum(pre_grad, axis=0).astype(jnp.bfloat16)
        slot_sum = jax.ops.segment_sum(pre_grad.reshape(-1, HID), slot_part.reshape(-1), num_segments=SLOTS).astype(jnp.bfloat16)
        grid_out = jnp.dot(grid_sum, w_grid, preferred_element_type=jnp.float32).astype(jnp.bfloat16)
        slot_out = jnp.dot(slot_sum, w_mesh, preferred_element_type=jnp.float32)
        collected = collected.at[node_list].add(slot_out)
        return collected, grid_out

    start = jnp.zeros((MESH, LAT), jnp.float32)
    collected, grid_out = lax.scan(per_owner, start, (grid_rows, edge_rows, slot_rows, node_table))
    return grid_out.reshape(GRID, LAT), collected.astype(jnp.bfloat16)
```

```python
import functools

import jax
import jax.numpy as jnp
from jax import lax
from jax.experimental import pallas as pl
from jax.experimental.pallas import tpu as pltpu
from jax.sharding import PartitionSpec as P

MESH_ID = pl.DeviceIdType.MESH
BF16 = jnp.bfloat16
F32 = jnp.float32
CHUNKS = 4
LANES = 128


def dot(a, b):
    return jnp.dot(a, b, preferred_element_type=F32)


def dot_nt(a, b):
    return lax.dot_general(a, b, (((1,), (1,)), ((), ())), preferred_element_type=F32)


def one_hot(cond):
    return jnp.where(cond, 1.0, 0.0).astype(BF16)


def as_column(row):
    return jnp.transpose(jnp.broadcast_to(row, (LANES, LANES)))


def slope_of(x):
    t = jnp.tanh(0.5 * x)
    sigma = 0.5 + 0.5 * t
    return sigma * (1.0 + x * (1.0 - sigma))


def kernel(
    dims,
    grid_hbm, mesh_hbm, cot_hbm, edge_hbm, slot_ref, serve_ref,
    wg_hbm, wm_hbm, we_hbm, wo_hbm, bias_ref,
    gout_hbm, mout_hbm,
    grid_v, mesh_v, cot_v, edge_v, wg_v, wm_v, we_v, wo_v,
    pick, tab_out, tab_in, serve_out, serve_in,
    wg_own, wg_sib, wm_out, wm_in,
    base_v, pre_v, hot, hot_t, gs_own, gs_sib, part_own, y_out, y_in,
    slot_out, slot_in, ret_out, ret_in, gout_v, mout_v,
    load_sem, edge_sem, store_sem,
    serve_s, serve_r, wg_s, wg_r, wm_s, wm_r, tab_s, tab_r,
    gs_s, gs_r, y_s, y_r, slot_s, slot_r, ret_s, ret_r,
):
    n_phase, n_blk, n_tp = dims
    n_y = n_tp // 2
    s, b, t = lax.axis_index("phase"), lax.axis_index("blk"), lax.axis_index("tp")
    y, core = lax.div(t, 2), lax.rem(t, 2)
    epg, rows, _ = edge_v.shape
    step = rows // CHUNKS
    nodes = mesh_v.shape[0]
    cap = serve_ref.shape[3]
    slots = n_blk * cap
    hid = wg_v.shape[0]
    feat = wg_own.shape[2]

    loads = []
    for i, (src, dst) in enumerate(
        [(mesh_hbm, mesh_v), (wm_hbm, wm_v), (cot_hbm, cot_v), (wo_hbm, wo_v),
         (wg_hbm, wg_v), (we_hbm, we_v), (grid_hbm, grid_v)]
    ):
        copy = pltpu.make_async_copy(src, dst, load_sem.at[i])
        copy.start()
        loads.append(copy)
    mesh_ld, wm_ld, cot_ld, wo_ld, wg_ld, we_ld, grid_ld = loads
    edge_ld = []
    for i in range(CHUNKS):
        part = pl.ds(i * step, step)
        copy = pltpu.make_async_copy(edge_hbm.at[:, part], edge_v.at[:, part], edge_sem.at[i])
        copy.start()
        edge_ld.append(copy)

    def remote(src, dst, send, recv, where):
        return pltpu.make_async_remote_copy(
            src_ref=src, dst_ref=dst, send_sem=send, recv_sem=recv,
            device_id=where, device_id_type=MESH_ID)

    barrier = pltpu.get_barrier_semaphore()
    others = [(i, j) for i in range(n_phase) for j in range(n_blk) if i or j]

    def shifted(i, j):
        return {"phase": lax.rem(s + i, n_phase), "blk": lax.rem(b + j, n_blk)}

    for d in range(1, n_tp):
        pl.semaphore_signal(barrier, inc=1, device_id={"tp": lax.rem(t + d, n_tp)}, device_id_type=MESH_ID)
    for i, j in others:
        pl.semaphore_signal(barrier, inc=1, device_id=shifted(i, j), device_id_type=MESH_ID)

    lane = lax.broadcasted_iota(jnp.int32, (LANES, LANES), 1)

    serve_row = jnp.concatenate([serve_ref[0, 0, i:i + 1, :] for i in range(n_blk)], axis=1)
    serve_out[...] = jnp.broadcast_to(serve_row, serve_out.shape)
    for i in range(slots // LANES):
        column = as_column(serve_row[:, i * LANES:(i + 1) * LANES])
        for j in range(nodes // LANES):
            pick[i * LANES:(i + 1) * LANES, j * LANES:(j + 1) * LANES] = one_hot(column == lane + j * LANES)
    mesh_ld.wait()
    lat = dot(pick[...], mesh_v[...]).astype(BF16)
    wm_ld.wait()
    mesh_pre = dot_nt(lat, wm_v[...]).astype(BF16)
    cot_ld.wait()
    cot = dot(pick[...], cot_v[...]).astype(BF16)
    wo_ld.wait()
    act = dot_nt(cot, wo_v[...]).astype(BF16)
    tab_out[:, :, :hid] = mesh_pre.reshape(n_blk, cap, hid)
    tab_out[:, :, hid:] = act.reshape(n_blk, cap, hid)
    tab_in[b] = tab_out[b]

    pl.semaphore_wait(barrier, n_tp - 1 + len(others))

    sends = []

    def send(copy):
        copy.start()
        sends.append(copy)
        return copy

    tab_cp = []
    for d in range(1, n_blk):
        to = lax.rem(b + d, n_blk)
        tab_cp.append(send(remote(tab_out.at[to], tab_in.at[b], tab_s.at[d], tab_r.at[d], {"blk": to})))

    wg_ld.wait()
    for j in range(n_tp):
        wg_own[j] = wg_v[:, j * feat:(j + 1) * feat]
        wm_out[j] = wm_v[:, j * feat:(j + 1) * feat]
    wm_in[t] = wm_out[t]
    sibling = {"tp": 2 * y + 1 - core}
    wg_cp = send(remote(wg_own, wg_sib, wg_s, wg_r, sibling))
    wm_cp = []
    for d in range(1, n_tp):
        to = lax.rem(t + d, n_tp)
        wm_cp.append(send(remote(wm_out.at[to], wm_in.at[t], wm_s.at[d], wm_r.at[d], {"tp": to})))
    serve_in[s] = serve_out[...]
    serve_cp = []
    for d in range(1, n_phase):
        to = lax.rem(s + d, n_phase)
        serve_cp.append(send(remote(serve_out, serve_in.at[s], serve_s.at[d], serve_r.at[d], {"phase": to})))

    def hot_body(i, carry):
        at = pl.ds(pl.multiple_of(i * LANES, LANES), LANES)
        for k in range(epg):
            row = slot_ref[k:k + 1, at]
            column = as_column(row)
            for j in range(slots // LANES):
                hot[k, at, j * LANES:(j + 1) * LANES] = one_hot(column == lane + j * LANES)
            hot_t[k, :, at] = one_hot(lax.broadcasted_iota(jnp.int32, (slots, LANES), 0) == row)
        return carry

    lax.fori_loop(0, rows // LANES, hot_body, 0)

    we_ld.wait()
    grid_ld.wait()
    for i in range(CHUNKS):
        edge_ld[i].wait()
        part = slice(i * step, (i + 1) * step)
        base_v[part, :] = dot_nt(grid_v[part, :], wg_v[...])
        for k in range(epg):
            pre_v[k, part, :] = dot_nt(edge_v[k, part, :], we_v[...])

    for cp in tab_cp:
        cp.wait_recv()
    table = tab_in[...].reshape(slots, 2 * hid)

    gs_cp, y_cp = [], []

    def cross(i):
        gs_cp[i].wait_recv()
        mine, theirs = gs_own[i], gs_sib[i]
        for d in range(n_y):
            to = 2 * lax.rem(y + d, n_y) + core
            share = dot(mine, wg_own[to]) + dot(theirs, wg_sib[to])
            if d == 0:
                part_own[i] = share
            else:
                y_out[d - 1, i] = share.astype(BF16)
                y_cp.append((d, i, send(remote(
                    y_out.at[d - 1, i], y_in.at[d - 1, i], y_s.at[d - 1, i], y_r.at[d - 1, i], {"tp": to}))))

    slot_total = jnp.zeros((slots, hid), F32)
    for i in range(CHUNKS):
        part = slice(i * step, (i + 1) * step)
        total = jnp.zeros((step, hid), F32)
        base = base_v[part, :] + bias_ref[...]
        for k in range(epg):
            got = dot(hot[k, part, :], table)
            slope = slope_of(pre_v[k, part, :] + base + got[:, :hid])
            total = total + got[:, hid:] * slope
            slot_total = slot_total + dot(hot_t[k, :, part], slope.astype(BF16))
        gs_own[i] = total.astype(BF16)
        gs_cp.append(send(remote(gs_own.at[i], gs_sib.at[i], gs_s.at[i], gs_r.at[i], sibling)))
        if i == 0:
            wg_cp.wait_recv()
        else:
            cross(i - 1)

    slot_out[...] = (slot_total * table[:, hid:].astype(F32)).astype(BF16)
    slot_in[t] = slot_out[...]
    slot_cp = []
    for d in range(1, n_tp):
        slot_cp.append(send(remote(
            slot_out, slot_in.at[t], slot_s.at[d], slot_r.at[d], {"tp": lax.rem(t + d, n_tp)})))
    cross(CHUNKS - 1)

    for cp in wm_cp:
        cp.wait_recv()
    for cp in slot_cp:
        cp.wait_recv()
    share = dot(slot_in[0], wm_in[0])
    for j in range(1, n_tp):
        share = share + dot(slot_in[j], wm_in[j])
    ret_out[...] = share.astype(BF16).reshape(n_blk, cap, feat)
    ret_in[s, b] = ret_out[b]
    ret_cp = []
    for n, (i, j) in enumerate(others):
        where = shifted(i, j)
        ret_cp.append(send(remote(
            ret_out.at[where["blk"]], ret_in.at[s, b], ret_s.at[n], ret_r.at[n], where)))

    stores = []
    for i in range(CHUNKS):
        value = part_own[i]
        for d, at, cp in y_cp:
            if at == i:
                cp.wait_recv()
                value = value + y_in[d - 1, i].astype(F32)
        part = pl.ds(i * step, step)
        gout_v[i * step:(i + 1) * step, :] = value.astype(BF16)
        copy = pltpu.make_async_copy(gout_v.at[part], gout_hbm.at[part], store_sem.at[i])
        copy.start()
        stores.append(copy)

    for cp in serve_cp:
        cp.wait_recv()
    for cp in ret_cp:
        cp.wait_recv()
    node = lax.broadcasted_iota(jnp.int32, (nodes, slots), 0)
    value = None
    for i in range(n_phase):
        spread = one_hot(node == serve_in[i, 0:1, :])
        more = dot(spread, ret_in[i].reshape(slots, feat))
        value = more if value is None else value + more
    mout_v[...] = value.astype(BF16)
    copy = pltpu.make_async_copy(mout_v, mout_hbm, store_sem.at[CHUNKS])
    copy.start()
    stores.append(copy)

    for cp in sends:
        cp.wait_send()
    for copy in stores:
        copy.wait()


def per_device(dims, grid_lat, mesh_lat, mesh_cot, edge_lat, edge_slot, serve_list, w_grid, w_mesh, w_edge, w_out, bias):
    n_phase, n_blk, n_tp = dims
    n_y = n_tp // 2
    epg, rows, lat = edge_lat.shape
    nodes = mesh_lat.shape[0]
    cap = serve_list.shape[3]
    slots = n_blk * cap
    hid = w_grid.shape[0]
    feat = lat // n_tp
    step = rows // CHUNKS
    n_other = n_phase * n_blk - 1
    vmem = pltpu.VMEM
    dma = pltpu.SemaphoreType.DMA
    hbm_spec = pl.BlockSpec(memory_space=pl.ANY)
    vmem_spec = pl.BlockSpec(memory_space=pltpu.VMEM)
    return pl.pallas_call(
        functools.partial(kernel, dims),
        out_shape=(
            jax.ShapeDtypeStruct((rows, feat), BF16),
            jax.ShapeDtypeStruct((nodes, feat), BF16),
        ),
        in_specs=[hbm_spec] * 4 + [vmem_spec] * 2 + [hbm_spec] * 4 + [vmem_spec],
        out_specs=(hbm_spec, hbm_spec),
        scratch_shapes=[
            vmem((rows, lat), BF16), vmem((nodes, lat), BF16), vmem((nodes, lat), BF16),
            vmem((epg, rows, lat), BF16),
            vmem((hid, lat), BF16), vmem((hid, lat), BF16), vmem((hid, lat), BF16), vmem((hid, lat), BF16),
            vmem((slots, nodes), BF16),
            vmem((n_blk, cap, 2 * hid), BF16), vmem((n_blk, cap, 2 * hid), BF16),
            vmem((8, slots), jnp.int32), vmem((n_phase, 8, slots), jnp.int32),
            vmem((n_tp, hid, feat), BF16), vmem((n_tp, hid, feat), BF16),
            vmem((n_tp, hid, feat), BF16), vmem((n_tp, hid, feat), BF16),
            vmem((rows, hid), F32), vmem((epg, rows, hid), F32),
            vmem((epg, rows, slots), BF16), vmem((epg, slots, rows), BF16),
            vmem((CHUNKS, step, hid), BF16), vmem((CHUNKS, step, hid), BF16),
            vmem((CHUNKS, step, feat), F32),
            vmem((max(n_y - 1, 1), CHUNKS, step, feat), BF16), vmem((max(n_y - 1, 1), CHUNKS, step, feat), BF16),
            vmem((slots, hid), BF16), vmem((n_tp, slots, hid), BF16),
            vmem((n_blk, cap, feat), BF16), vmem((n_phase, n_blk, cap, feat), BF16),
            vmem((rows, feat), BF16), vmem((nodes, feat), BF16),
            dma((7,)), dma((CHUNKS,)), dma((CHUNKS + 1,)),
            dma((n_phase,)), dma((n_phase,)), dma, dma, dma((n_tp,)), dma((n_tp,)), dma((n_blk,)), dma((n_blk,)),
            dma((CHUNKS,)), dma((CHUNKS,)), dma((max(n_y - 1, 1), CHUNKS)), dma((max(n_y - 1, 1), CHUNKS)),
            dma((n_tp,)), dma((n_tp,)), dma((n_other,)), dma((n_other,)),
        ],
        compiler_params=pltpu.CompilerParams(
            collective_id=0, has_side_effects=True, vmem_limit_bytes=56 * 1024 * 1024),
    )(grid_lat, mesh_lat, mesh_cot, edge_lat, edge_slot, serve_list,
      w_grid, w_mesh, w_edge, w_out, bias.reshape(1, hid))


def solution(mesh):
    dims = (mesh.shape["phase"], mesh.shape["blk"], mesh.shape["tp"])
    in_specs = (
        P(("phase", "blk"), None),
        P("blk", None),
        P("blk", None),
        P(None, ("phase", "blk"), None),
        P(None, ("phase", "blk")),
        P("phase", "blk", None, None),
        P("tp", None),
        P("tp", None),
        P("tp", None),
        P("tp", None),
        P("tp"),
    )
    out_specs = (P(("phase", "blk"), "tp"), P("blk", "tp"))
    return jax.shard_map(
        functools.partial(per_device, dims), mesh=mesh, in_specs=in_specs, out_specs=out_specs, check_vma=False
    )
```

```python
import functools

import jax
import jax.numpy as jnp
from jax import lax
from jax.experimental import pallas as pl
from jax.experimental.pallas import tpu as pltpu
from jax.sharding import PartitionSpec as P

MESH_ID = pl.DeviceIdType.MESH
BF16 = jnp.bfloat16
F32 = jnp.float32
CHUNKS = 4
LANES = 128


def dot(a, b):
    return jnp.dot(a, b, preferred_element_type=F32)


def dot_nt(a, b):
    return lax.dot_general(a, b, (((1,), (1,)), ((), ())), preferred_element_type=F32)


def one_hot(cond):
    return jnp.where(cond, 1.0, 0.0).astype(BF16)


def as_column(row):
    return jnp.transpose(jnp.broadcast_to(row, (LANES, LANES)))


def slope_of(x):
    t = jnp.tanh(0.5 * x)
    sigma = 0.5 + 0.5 * t
    return sigma * (1.0 + x * (1.0 - sigma))


def kernel(
    dims,
    grid_hbm, mesh_hbm, cot_hbm, edge_hbm, slot_ref, serve_ref,
    wg_hbm, wm_hbm, we_hbm, wo_hbm, bias_ref,
    gout_hbm, mout_hbm,
    grid_v, mesh_v, cot_v, edge_v, wg_v, wm_v, we_v, wo_v,
    pick, tab_out, tab_in, serve_out, serve_in,
    wg_own, wg_sib, wm_out, wm_in,
    base_v, pre_v, hot, hot_t, gs_own, gs_sib, part_own, y_out, y_in,
    slot_out, slot_in, ret_out, ret_in, gout_v, mout_v,
    load_sem, edge_sem, store_sem,
    serve_s, serve_r, wg_s, wg_r, wm_s, wm_r, tab_s, tab_r,
    gs_s, gs_r, y_s, y_r, slot_s, slot_r, ret_s, ret_r,
):
    n_phase, n_blk, n_tp = dims
    n_y = n_tp // 2
    s, b, t = lax.axis_index("phase"), lax.axis_index("blk"), lax.axis_index("tp")
    y, core = lax.div(t, 2), lax.rem(t, 2)
    epg, rows, _ = edge_v.shape
    step = rows // CHUNKS
    nodes = mesh_v.shape[0]
    cap = serve_ref.shape[3]
    slots = n_blk * cap
    hid = wg_v.shape[0]
    feat = wg_own.shape[2]

    loads = []
    for i, (src, dst) in enumerate(
        [(mesh_hbm, mesh_v), (wm_hbm, wm_v), (cot_hbm, cot_v), (wo_hbm, wo_v),
         (wg_hbm, wg_v), (we_hbm, we_v), (grid_hbm, grid_v)]
    ):
        copy = pltpu.make_async_copy(src, dst, load_sem.at[i])
        copy.start()
        loads.append(copy)
    mesh_ld, wm_ld, cot_ld, wo_ld, wg_ld, we_ld, grid_ld = loads
    edge_ld = []
    for i in range(CHUNKS):
        part = pl.ds(i * step, step)
        copy = pltpu.make_async_copy(edge_hbm.at[:, part], edge_v.at[:, part], edge_sem.at[i])
        copy.start()
        edge_ld.append(copy)

    def remote(src, dst, send, recv, where):
        return pltpu.make_async_remote_copy(
            src_ref=src, dst_ref=dst, send_sem=send, recv_sem=recv,
            device_id=where, device_id_type=MESH_ID)

    barrier = pltpu.get_barrier_semaphore()
    others = [(i, j) for i in range(n_phase) for j in range(n_blk) if i or j]

    def shifted(i, j):
        return {"phase": lax.rem(s + i, n_phase), "blk": lax.rem(b + j, n_blk)}

    for d in range(1, n_tp):
        pl.semaphore_signal(barrier, inc=1, device_id={"tp": lax.rem(t + d, n_tp)}, device_id_type=MESH_ID)
    for i, j in others:
        pl.semaphore_signal(barrier, inc=1, device_id=shifted(i, j), device_id_type=MESH_ID)

    lane = lax.broadcasted_iota(jnp.int32, (LANES, LANES), 1)

    serve_row = jnp.concatenate([serve_ref[0, 0, i:i + 1, :] for i in range(n_blk)], axis=1)
    serve_out[...] = jnp.broadcast_to(serve_row, serve_out.shape)
    for i in range(slots // LANES):
        column = as_column(serve_row[:, i * LANES:(i + 1) * LANES])
        for j in range(nodes // LANES):
            pick[i * LANES:(i + 1) * LANES, j * LANES:(j + 1) * LANES] = one_hot(column == lane + j * LANES)
    mesh_ld.wait()
    lat = dot(pick[...], mesh_v[...]).astype(BF16)
    wm_ld.wait()
    mesh_pre = dot_nt(lat, wm_v[...]).astype(BF16)
    cot_ld.wait()
    cot = dot(pick[...], cot_v[...]).astype(BF16)
    wo_ld.wait()
    act = dot_nt(cot, wo_v[...]).astype(BF16)
    tab_out[:, :, :hid] = mesh_pre.reshape(n_blk, cap, hid)
    tab_out[:, :, hid:] = act.reshape(n_blk, cap, hid)
    tab_in[b] = tab_out[b]

    pl.semaphore_wait(barrier, n_tp - 1 + len(others))

    sends = []

    def send(copy):
        copy.start()
        sends.append(copy)
        return copy

    tab_cp = []
    for d in range(1, n_blk):
        to = lax.rem(b + d, n_blk)
        tab_cp.append(send(remote(tab_out.at[to], tab_in.at[b], tab_s.at[d], tab_r.at[d], {"blk": to})))

    wg_ld.wait()
    for j in range(n_tp):
        wg_own[j] = wg_v[:, j * feat:(j + 1) * feat]
        wm_out[j] = wm_v[:, j * feat:(j + 1) * feat]
    wm_in[t] = wm_out[t]
    sibling = {"tp": 2 * y + 1 - core}
    wg_cp = send(remote(wg_own, wg_sib, wg_s, wg_r, sibling))
    wm_cp = []
    for d in range(1, n_tp):
        to = lax.rem(t + d, n_tp)
        wm_cp.append(send(remote(wm_out.at[to], wm_in.at[t], wm_s.at[d], wm_r.at[d], {"tp": to})))
    serve_in[s] = serve_out[...]
    serve_cp = []
    for d in range(1, n_phase):
        to = lax.rem(s + d, n_phase)
        serve_cp.append(send(remote(serve_out, serve_in.at[s], serve_s.at[d], serve_r.at[d], {"phase": to})))

    def hot_body(i, carry):
        at = pl.ds(pl.multiple_of(i * LANES, LANES), LANES)
        for k in range(epg):
            row = slot_ref[k:k + 1, at]
            column = as_column(row)
            for j in range(slots // LANES):
                hot[k, at, j * LANES:(j + 1) * LANES] = one_hot(column == lane + j * LANES)
            hot_t[k, :, at] = one_hot(lax.broadcasted_iota(jnp.int32, (slots, LANES), 0) == row)
        return carry

    lax.fori_loop(0, rows // LANES, hot_body, 0)

    we_ld.wait()
    grid_ld.wait()
    for i in range(CHUNKS):
        edge_ld[i].wait()
        part = slice(i * step, (i + 1) * step)
        base_v[part, :] = dot_nt(grid_v[part, :], wg_v[...])
        for k in range(epg):
            pre_v[k, part, :] = dot_nt(edge_v[k, part, :], we_v[...])

    for cp in tab_cp:
        cp.wait_recv()
    table = tab_in[...].reshape(slots, 2 * hid)

    gs_cp, y_cp = [], []

    def cross(i):
        gs_cp[i].wait_recv()
        mine, theirs = gs_own[i], gs_sib[i]
        for d in range(n_y):
            to = 2 * lax.rem(y + d, n_y) + core
            share = dot(mine, wg_own[to]) + dot(theirs, wg_sib[to])
            if d == 0:
                part_own[i] = share
            else:
                y_out[d - 1, i] = share.astype(BF16)
                y_cp.append((d, i, send(remote(
                    y_out.at[d - 1, i], y_in.at[d - 1, i], y_s.at[d - 1, i], y_r.at[d - 1, i], {"tp": to}))))

    slot_total = jnp.zeros((slots, hid), F32)
    for i in range(CHUNKS):
        part = slice(i * step, (i + 1) * step)
        total = jnp.zeros((step, hid), F32)
        base = base_v[part, :] + bias_ref[...]
        for k in range(epg):
            got = dot(hot[k, part, :], table)
            slope = slope_of(pre_v[k, part, :] + base + got[:, :hid])
            total = total + got[:, hid:] * slope
            slot_total = slot_total + dot(hot_t[k, :, part], slope.astype(BF16))
        gs_own[i] = total.astype(BF16)
        gs_cp.append(send(remote(gs_own.at[i], gs_sib.at[i], gs_s.at[i], gs_r.at[i], sibling)))

    slot_out[...] = (slot_total * table[:, hid:].astype(F32)).astype(BF16)
    slot_in[t] = slot_out[...]
    slot_cp = []
    for d in range(1, n_tp):
        slot_cp.append(send(remote(
            slot_out, slot_in.at[t], slot_s.at[d], slot_r.at[d], {"tp": lax.rem(t + d, n_tp)})))
    wg_cp.wait_recv()
    for i in range(CHUNKS):
        cross(i)

    for cp in wm_cp:
        cp.wait_recv()
    for cp in slot_cp:
        cp.wait_recv()
    share = dot(slot_in[0], wm_in[0])
    for j in range(1, n_tp):
        share = share + dot(slot_in[j], wm_in[j])
    ret_out[...] = share.astype(BF16).reshape(n_blk, cap, feat)
    ret_in[s, b] = ret_out[b]
    ret_cp = []
    for n, (i, j) in enumerate(others):
        where = shifted(i, j)
        ret_cp.append(send(remote(
            ret_out.at[where["blk"]], ret_in.at[s, b], ret_s.at[n], ret_r.at[n], where)))

    stores = []
    for i in range(CHUNKS):
        value = part_own[i]
        for d, at, cp in y_cp:
            if at == i:
                cp.wait_recv()
                value = value + y_in[d - 1, i].astype(F32)
        part = pl.ds(i * step, step)
        gout_v[i * step:(i + 1) * step, :] = value.astype(BF16)
        copy = pltpu.make_async_copy(gout_v.at[part], gout_hbm.at[part], store_sem.at[i])
        copy.start()
        stores.append(copy)

    for cp in serve_cp:
        cp.wait_recv()
    for cp in ret_cp:
        cp.wait_recv()
    node = lax.broadcasted_iota(jnp.int32, (nodes, slots), 0)
    value = None
    for i in range(n_phase):
        spread = one_hot(node == serve_in[i, 0:1, :])
        more = dot(spread, ret_in[i].reshape(slots, feat))
        value = more if value is None else value + more
    mout_v[...] = value.astype(BF16)
    copy = pltpu.make_async_copy(mout_v, mout_hbm, store_sem.at[CHUNKS])
    copy.start()
    stores.append(copy)

    for cp in sends:
        cp.wait_send()
    for copy in stores:
        copy.wait()


def tail_kernel(grid_ref, mesh_ref, grid_out, mesh_out):
    grid_out[...] = grid_ref[...]
    mesh_out[...] = mesh_ref[...]


def per_device(dims, grid_lat, mesh_lat, mesh_cot, edge_lat, edge_slot, serve_list, w_grid, w_mesh, w_edge, w_out, bias):
    n_phase, n_blk, n_tp = dims
    n_y = n_tp // 2
    epg, rows, lat = edge_lat.shape
    nodes = mesh_lat.shape[0]
    cap = serve_list.shape[3]
    slots = n_blk * cap
    hid = w_grid.shape[0]
    feat = lat // n_tp
    step = rows // CHUNKS
    n_other = n_phase * n_blk - 1
    vmem = pltpu.VMEM
    dma = pltpu.SemaphoreType.DMA
    hbm_spec = pl.BlockSpec(memory_space=pl.ANY)
    vmem_spec = pl.BlockSpec(memory_space=pltpu.VMEM)
    grid_out, mesh_out = pl.pallas_call(
        functools.partial(kernel, dims),
        out_shape=(
            jax.ShapeDtypeStruct((rows, feat), BF16),
            jax.ShapeDtypeStruct((nodes, feat), BF16),
        ),
        in_specs=[hbm_spec] * 4 + [vmem_spec] * 2 + [hbm_spec] * 4 + [vmem_spec],
        out_specs=(hbm_spec, hbm_spec),
        scratch_shapes=[
            vmem((rows, lat), BF16), vmem((nodes, lat), BF16), vmem((nodes, lat), BF16),
            vmem((epg, rows, lat), BF16),
            vmem((hid, lat), BF16), vmem((hid, lat), BF16), vmem((hid, lat), BF16), vmem((hid, lat), BF16),
            vmem((slots, nodes), BF16),
            vmem((n_blk, cap, 2 * hid), BF16), vmem((n_blk, cap, 2 * hid), BF16),
            vmem((8, slots), jnp.int32), vmem((n_phase, 8, slots), jnp.int32),
            vmem((n_tp, hid, feat), BF16), vmem((n_tp, hid, feat), BF16),
            vmem((n_tp, hid, feat), BF16), vmem((n_tp, hid, feat), BF16),
            vmem((rows, hid), F32), vmem((epg, rows, hid), F32),
            vmem((epg, rows, slots), BF16), vmem((epg, slots, rows), BF16),
            vmem((CHUNKS, step, hid), BF16), vmem((CHUNKS, step, hid), BF16),
            vmem((CHUNKS, step, feat), F32),
            vmem((max(n_y - 1, 1), CHUNKS, step, feat), BF16), vmem((max(n_y - 1, 1), CHUNKS, step, feat), BF16),
            vmem((slots, hid), BF16), vmem((n_tp, slots, hid), BF16),
            vmem((n_blk, cap, feat), BF16), vmem((n_phase, n_blk, cap, feat), BF16),
            vmem((rows, feat), BF16), vmem((nodes, feat), BF16),
            dma((7,)), dma((CHUNKS,)), dma((CHUNKS + 1,)),
            dma((n_phase,)), dma((n_phase,)), dma, dma, dma((n_tp,)), dma((n_tp,)), dma((n_blk,)), dma((n_blk,)),
            dma((CHUNKS,)), dma((CHUNKS,)), dma((max(n_y - 1, 1), CHUNKS)), dma((max(n_y - 1, 1), CHUNKS)),
            dma((n_tp,)), dma((n_tp,)), dma((n_other,)), dma((n_other,)),
        ],
        compiler_params=pltpu.CompilerParams(
            collective_id=0, has_side_effects=True, vmem_limit_bytes=56 * 1024 * 1024),
    )(grid_lat, mesh_lat, mesh_cot, edge_lat, edge_slot, serve_list,
      w_grid, w_mesh, w_edge, w_out, bias.reshape(1, hid))
    return pl.pallas_call(
        tail_kernel,
        out_shape=(
            jax.ShapeDtypeStruct((rows, feat), BF16),
            jax.ShapeDtypeStruct((nodes, feat), BF16),
        ),
        in_specs=[vmem_spec] * 2,
        out_specs=(vmem_spec, vmem_spec),
    )(grid_out, mesh_out)


def solution(mesh):
    dims = (mesh.shape["phase"], mesh.shape["blk"], mesh.shape["tp"])
    in_specs = (
        P(("phase", "blk"), None),
        P("blk", None),
        P("blk", None),
        P(None, ("phase", "blk"), None),
        P(None, ("phase", "blk")),
        P("phase", "blk", None, None),
        P("tp", None),
        P("tp", None),
        P("tp", None),
        P("tp", None),
        P("tp"),
    )
    out_specs = (P(("phase", "blk"), "tp"), P("blk", "tp"))
    return jax.shard_map(
        functools.partial(per_device, dims), mesh=mesh, in_specs=in_specs, out_specs=out_specs, check_vma=False
    )
```

```python
import functools

import jax
import jax.numpy as jnp
from jax import lax
from jax.experimental import pallas as pl
from jax.experimental.pallas import tpu as pltpu
from jax.sharding import PartitionSpec as P

MESH_ID = pl.DeviceIdType.MESH
BF16 = jnp.bfloat16
F32 = jnp.float32
CHUNKS = 4
LANES = 128


def dot(a, b):
    return jnp.dot(a, b, preferred_element_type=F32)


def dot_nt(a, b):
    return lax.dot_general(a, b, (((1,), (1,)), ((), ())), preferred_element_type=F32)


def one_hot(cond):
    return jnp.where(cond, 1.0, 0.0).astype(BF16)


def as_column(row):
    return jnp.transpose(jnp.broadcast_to(row, (LANES, LANES)))


def slope_of(x):
    t = jnp.tanh(0.5 * x)
    sigma = 0.5 + 0.5 * t
    return sigma * (1.0 + x * (1.0 - sigma))


def kernel(
    dims,
    grid_hbm, mesh_hbm, cot_hbm, edge_hbm, slot_ref, serve_ref,
    wg_hbm, wm_hbm, we_hbm, wo_hbm, bias_ref,
    gout_hbm, mout_hbm,
    grid_v, mesh_v, cot_v, edge_v, wg_v, wm_v, we_v, wo_v,
    pick, tab_out, tab_in, serve_out, serve_in,
    wg_own, wg_sib, wm_out, wm_in,
    base_v, pre_v, hot, hot_t, got_v, slope_v, gs_own, gs_sib, part_own, y_out, y_in,
    slot_out, slot_in, ret_out, ret_in, gout_v, mout_v,
    load_sem, edge_sem, store_sem,
    serve_s, serve_r, wg_s, wg_r, wm_s, wm_r, tab_s, tab_r,
    gs_s, gs_r, y_s, y_r, slot_s, slot_r, ret_s, ret_r,
):
    n_phase, n_blk, n_tp = dims
    n_y = n_tp // 2
    s, b, t = lax.axis_index("phase"), lax.axis_index("blk"), lax.axis_index("tp")
    y, core = lax.div(t, 2), lax.rem(t, 2)
    epg, rows, _ = edge_v.shape
    step = rows // CHUNKS
    nodes = mesh_v.shape[0]
    cap = serve_ref.shape[3]
    slots = n_blk * cap
    hid = wg_v.shape[0]
    feat = wg_own.shape[2]

    loads = []
    for i, (src, dst) in enumerate(
        [(mesh_hbm, mesh_v), (wm_hbm, wm_v), (cot_hbm, cot_v), (wo_hbm, wo_v),
         (wg_hbm, wg_v), (we_hbm, we_v), (grid_hbm, grid_v)]
    ):
        copy = pltpu.make_async_copy(src, dst, load_sem.at[i])
        copy.start()
        loads.append(copy)
    mesh_ld, wm_ld, cot_ld, wo_ld, wg_ld, we_ld, grid_ld = loads
    edge_ld = []
    for i in range(CHUNKS):
        part = pl.ds(i * step, step)
        copy = pltpu.make_async_copy(edge_hbm.at[:, part], edge_v.at[:, part], edge_sem.at[i])
        copy.start()
        edge_ld.append(copy)

    def remote(src, dst, send, recv, where):
        return pltpu.make_async_remote_copy(
            src_ref=src, dst_ref=dst, send_sem=send, recv_sem=recv,
            device_id=where, device_id_type=MESH_ID)

    barrier = pltpu.get_barrier_semaphore()
    others = [(i, j) for i in range(n_phase) for j in range(n_blk) if i or j]

    def shifted(i, j):
        return {"phase": lax.rem(s + i, n_phase), "blk": lax.rem(b + j, n_blk)}

    for d in range(1, n_tp):
        pl.semaphore_signal(barrier, inc=1, device_id={"tp": lax.rem(t + d, n_tp)}, device_id_type=MESH_ID)
    for i, j in others:
        pl.semaphore_signal(barrier, inc=1, device_id=shifted(i, j), device_id_type=MESH_ID)

    lane = lax.broadcasted_iota(jnp.int32, (LANES, LANES), 1)

    serve_row = jnp.concatenate([serve_ref[0, 0, i:i + 1, :] for i in range(n_blk)], axis=1)
    serve_out[...] = jnp.broadcast_to(serve_row, serve_out.shape)
    for i in range(slots // LANES):
        column = as_column(serve_row[:, i * LANES:(i + 1) * LANES])
        for j in range(nodes // LANES):
            pick[i * LANES:(i + 1) * LANES, j * LANES:(j + 1) * LANES] = one_hot(column == lane + j * LANES)
    mesh_ld.wait()
    lat = dot(pick[...], mesh_v[...]).astype(BF16)
    wm_ld.wait()
    mesh_pre = dot_nt(lat, wm_v[...]).astype(BF16)
    cot_ld.wait()
    cot = dot(pick[...], cot_v[...]).astype(BF16)
    wo_ld.wait()
    act = dot_nt(cot, wo_v[...]).astype(BF16)
    tab_out[:, :, :hid] = mesh_pre.reshape(n_blk, cap, hid)
    tab_out[:, :, hid:] = act.reshape(n_blk, cap, hid)
    tab_in[b] = tab_out[b]

    pl.semaphore_wait(barrier, n_tp - 1 + len(others))

    sends = []

    def send(copy):
        copy.start()
        sends.append(copy)
        return copy

    tab_cp = []
    for d in range(1, n_blk):
        to = lax.rem(b + d, n_blk)
        tab_cp.append(send(remote(tab_out.at[to], tab_in.at[b], tab_s.at[d], tab_r.at[d], {"blk": to})))

    wg_ld.wait()
    for j in range(n_tp):
        wg_own[j] = wg_v[:, j * feat:(j + 1) * feat]
        wm_out[j] = wm_v[:, j * feat:(j + 1) * feat]
    wm_in[t] = wm_out[t]
    sibling = {"tp": 2 * y + 1 - core}
    wg_cp = send(remote(wg_own, wg_sib, wg_s, wg_r, sibling))
    wm_cp = []
    for d in range(1, n_tp):
        to = lax.rem(t + d, n_tp)
        wm_cp.append(send(remote(wm_out.at[to], wm_in.at[t], wm_s.at[d], wm_r.at[d], {"tp": to})))
    serve_in[s] = serve_out[...]
    serve_cp = []
    for d in range(1, n_phase):
        to = lax.rem(s + d, n_phase)
        serve_cp.append(send(remote(serve_out, serve_in.at[s], serve_s.at[d], serve_r.at[d], {"phase": to})))

    def hot_body(i, carry):
        at = pl.ds(pl.multiple_of(i * LANES, LANES), LANES)
        for k in range(epg):
            row = slot_ref[k:k + 1, at]
            column = as_column(row)
            for j in range(slots // LANES):
                hot[k, at, j * LANES:(j + 1) * LANES] = one_hot(column == lane + j * LANES)
            hot_t[:, pl.ds(pl.multiple_of(k * rows + i * LANES, LANES), LANES)] = one_hot(lax.broadcasted_iota(jnp.int32, (slots, LANES), 0) == row)
        return carry

    lax.fori_loop(0, rows // LANES, hot_body, 0)

    we_ld.wait()
    grid_ld.wait()
    for i in range(CHUNKS):
        edge_ld[i].wait()
        part = slice(i * step, (i + 1) * step)
        base_v[part, :] = dot_nt(grid_v[part, :], wg_v[...])
        for k in range(epg):
            pre_v[k, part, :] = dot_nt(edge_v[k, part, :], we_v[...])

    for cp in tab_cp:
        cp.wait_recv()
    table = tab_in[...].reshape(slots, 2 * hid)

    gs_cp, y_cp = [], []

    def cross(i):
        gs_cp[i].wait_recv()
        mine, theirs = gs_own[i], gs_sib[i]
        for d in range(n_y):
            to = 2 * lax.rem(y + d, n_y) + core
            share = dot(mine, wg_own[to]) + dot(theirs, wg_sib[to])
            if d == 0:
                part_own[i] = share
            else:
                y_out[d - 1, i] = share.astype(BF16)
                y_cp.append((d, i, send(remote(
                    y_out.at[d - 1, i], y_in.at[d - 1, i], y_s.at[d - 1, i], y_r.at[d - 1, i], {"tp": to}))))

    for k in range(epg):
        got_v[k] = dot(hot[k], table)
    for i in range(CHUNKS):
        part = slice(i * step, (i + 1) * step)
        total = jnp.zeros((step, hid), F32)
        base = base_v[part, :] + bias_ref[...]
        for k in range(epg):
            slope = slope_of(pre_v[k, part, :] + base + got_v[k, part, :hid])
            total = total + got_v[k, part, hid:] * slope
            slope_v[k * rows + i * step:k * rows + (i + 1) * step, :] = slope.astype(BF16)
        gs_own[i] = total.astype(BF16)
        gs_cp.append(send(remote(gs_own.at[i], gs_sib.at[i], gs_s.at[i], gs_r.at[i], sibling)))

    slot_total = dot(hot_t[...], slope_v[...])
    slot_out[...] = (slot_total * table[:, hid:].astype(F32)).astype(BF16)
    slot_in[t] = slot_out[...]
    slot_cp = []
    for d in range(1, n_tp):
        slot_cp.append(send(remote(
            slot_out, slot_in.at[t], slot_s.at[d], slot_r.at[d], {"tp": lax.rem(t + d, n_tp)})))
    wg_cp.wait_recv()
    for i in range(CHUNKS):
        cross(i)

    for cp in wm_cp:
        cp.wait_recv()
    for cp in slot_cp:
        cp.wait_recv()
    share = dot(slot_in[0], wm_in[0])
    for j in range(1, n_tp):
        share = share + dot(slot_in[j], wm_in[j])
    ret_out[...] = share.astype(BF16).reshape(n_blk, cap, feat)
    ret_in[s, b] = ret_out[b]
    ret_cp = []
    for n, (i, j) in enumerate(others):
        where = shifted(i, j)
        ret_cp.append(send(remote(
            ret_out.at[where["blk"]], ret_in.at[s, b], ret_s.at[n], ret_r.at[n], where)))

    stores = []
    for i in range(CHUNKS):
        value = part_own[i]
        for d, at, cp in y_cp:
            if at == i:
                cp.wait_recv()
                value = value + y_in[d - 1, i].astype(F32)
        part = pl.ds(i * step, step)
        gout_v[i * step:(i + 1) * step, :] = value.astype(BF16)
        copy = pltpu.make_async_copy(gout_v.at[part], gout_hbm.at[part], store_sem.at[i])
        copy.start()
        stores.append(copy)

    for cp in serve_cp:
        cp.wait_recv()
    for cp in ret_cp:
        cp.wait_recv()
    node = lax.broadcasted_iota(jnp.int32, (nodes, slots), 0)
    value = None
    for i in range(n_phase):
        spread = one_hot(node == serve_in[i, 0:1, :])
        more = dot(spread, ret_in[i].reshape(slots, feat))
        value = more if value is None else value + more
    mout_v[...] = value.astype(BF16)
    copy = pltpu.make_async_copy(mout_v, mout_hbm, store_sem.at[CHUNKS])
    copy.start()
    stores.append(copy)

    for cp in sends:
        cp.wait_send()
    for copy in stores:
        copy.wait()


def tail_kernel(grid_ref, mesh_ref, grid_out, mesh_out):
    grid_out[...] = grid_ref[...]
    mesh_out[...] = mesh_ref[...]


def per_device(dims, grid_lat, mesh_lat, mesh_cot, edge_lat, edge_slot, serve_list, w_grid, w_mesh, w_edge, w_out, bias):
    n_phase, n_blk, n_tp = dims
    n_y = n_tp // 2
    epg, rows, lat = edge_lat.shape
    nodes = mesh_lat.shape[0]
    cap = serve_list.shape[3]
    slots = n_blk * cap
    hid = w_grid.shape[0]
    feat = lat // n_tp
    step = rows // CHUNKS
    n_other = n_phase * n_blk - 1
    vmem = pltpu.VMEM
    dma = pltpu.SemaphoreType.DMA
    hbm_spec = pl.BlockSpec(memory_space=pl.ANY)
    vmem_spec = pl.BlockSpec(memory_space=pltpu.VMEM)
    grid_out, mesh_out = pl.pallas_call(
        functools.partial(kernel, dims),
        out_shape=(
            jax.ShapeDtypeStruct((rows, feat), BF16),
            jax.ShapeDtypeStruct((nodes, feat), BF16),
        ),
        in_specs=[hbm_spec] * 4 + [vmem_spec] * 2 + [hbm_spec] * 4 + [vmem_spec],
        out_specs=(hbm_spec, hbm_spec),
        scratch_shapes=[
            vmem((rows, lat), BF16), vmem((nodes, lat), BF16), vmem((nodes, lat), BF16),
            vmem((epg, rows, lat), BF16),
            vmem((hid, lat), BF16), vmem((hid, lat), BF16), vmem((hid, lat), BF16), vmem((hid, lat), BF16),
            vmem((slots, nodes), BF16),
            vmem((n_blk, cap, 2 * hid), BF16), vmem((n_blk, cap, 2 * hid), BF16),
            vmem((8, slots), jnp.int32), vmem((n_phase, 8, slots), jnp.int32),
            vmem((n_tp, hid, feat), BF16), vmem((n_tp, hid, feat), BF16),
            vmem((n_tp, hid, feat), BF16), vmem((n_tp, hid, feat), BF16),
            vmem((rows, hid), F32), vmem((epg, rows, hid), F32),
            vmem((epg, rows, slots), BF16), vmem((slots, epg * rows), BF16), vmem((epg, rows, 2 * hid), F32), vmem((epg * rows, hid), BF16),
            vmem((CHUNKS, step, hid), BF16), vmem((CHUNKS, step, hid), BF16),
            vmem((CHUNKS, step, feat), F32),
            vmem((max(n_y - 1, 1), CHUNKS, step, feat), BF16), vmem((max(n_y - 1, 1), CHUNKS, step, feat), BF16),
            vmem((slots, hid), BF16), vmem((n_tp, slots, hid), BF16),
            vmem((n_blk, cap, feat), BF16), vmem((n_phase, n_blk, cap, feat), BF16),
            vmem((rows, feat), BF16), vmem((nodes, feat), BF16),
            dma((7,)), dma((CHUNKS,)), dma((CHUNKS + 1,)),
            dma((n_phase,)), dma((n_phase,)), dma, dma, dma((n_tp,)), dma((n_tp,)), dma((n_blk,)), dma((n_blk,)),
            dma((CHUNKS,)), dma((CHUNKS,)), dma((max(n_y - 1, 1), CHUNKS)), dma((max(n_y - 1, 1), CHUNKS)),
            dma((n_tp,)), dma((n_tp,)), dma((n_other,)), dma((n_other,)),
        ],
        compiler_params=pltpu.CompilerParams(
            collective_id=0, has_side_effects=True, vmem_limit_bytes=56 * 1024 * 1024),
    )(grid_lat, mesh_lat, mesh_cot, edge_lat, edge_slot, serve_list,
      w_grid, w_mesh, w_edge, w_out, bias.reshape(1, hid))
    return pl.pallas_call(
        tail_kernel,
        out_shape=(
            jax.ShapeDtypeStruct((rows, feat), BF16),
            jax.ShapeDtypeStruct((nodes, feat), BF16),
        ),
        in_specs=[vmem_spec] * 2,
        out_specs=(vmem_spec, vmem_spec),
    )(grid_out, mesh_out)


def solution(mesh):
    dims = (mesh.shape["phase"], mesh.shape["blk"], mesh.shape["tp"])
    in_specs = (
        P(("phase", "blk"), None),
        P("blk", None),
        P("blk", None),
        P(None, ("phase", "blk"), None),
        P(None, ("phase", "blk")),
        P("phase", "blk", None, None),
        P("tp", None),
        P("tp", None),
        P("tp", None),
        P("tp", None),
        P("tp"),
    )
    out_specs = (P(("phase", "blk"), "tp"), P("blk", "tp"))
    return jax.shard_map(
        functools.partial(per_device, dims), mesh=mesh, in_specs=in_specs, out_specs=out_specs, check_vma=False
    )
```
